512 devices in a mesh: row: 16 (over y_hi, z), col: 8 (over y_lo, core), depth: 4 (over x).
Axes of the slice: x: 4, y: 8 (y_hi: 2, y_lo: 4; y = y_hi * 4 + y_lo), z: 8, core: 2. Of those that a mesh axis runs over, the one named last changes fastest.
Arguments:
- integrals: bfloat16 [4096, 16384], P('row', ('col', 'depth')), may hold values from -0.046875 to 0.046875
- amplitudes: bfloat16 [16384, 4096], P(('row', 'depth'), 'col'), may hold values from -6 to 6
Outputs:
- ladder: float32 [4096, 4096], P('row', ('col', 'depth'))
The draws below stay inside these ranges and needn't reach their ends.
All inputs are finite; a program needn't handle non-finite values.
Results may differ from the reference program's by a relative error of at most 0.0003.
Values may be sent and summed in bfloat16 or wider, within the bound.
No kernel may reach another device: no remote copies, remote signals or barrier semaphores. Data moves between devices by JAX's collectives and lax.ppermute only.
A program may use at most 64 MiB of HBM per device.

```python
import jax
import jax.numpy as jnp

IJ_PAIRS = 4096
SLAB_ROWS = 4096
CD_PAIRS = 16384


def block_levels(stream_key, shape, shards, smallest, high):
    factor_of = 1.0
    for dim, shards_of in shards:
        heights = jax.random.uniform(jax.random.fold_in(jax.random.fold_in(stream_key, 6), dim), (shards_of,), jnp.float32, smallest / len(shards), high / len(shards))
        factor_of = factor_of * jnp.repeat(jnp.exp(heights), shape[dim] // shards_of).reshape((-1,) + (1,) * (len(shape) - 1 - dim))
    return factor_of


def scatter_about(stream_key, shape, scale, reach, split=(), dtype=jnp.bfloat16):
    result = jax.random.normal(stream_key, shape, jnp.float32) * scale
    if len(split) > 0:
        result = block_levels(stream_key, shape, split, -0.22, 0.18) * result
    return jnp.clip(result, min=-reach, max=reach).astype(dtype)


def setup_inputs(seed: int = 0) -> dict:
    key_of = jax.random.split(jax.random.key(seed), 3)
    return {
        "integrals": scatter_about(key_of[0], (SLAB_ROWS, CD_PAIRS), CD_PAIRS ** -0.5, 0.046875, ((0, 16), (1, 32))),
        "amplitudes": scatter_about(key_of[1], (CD_PAIRS, IJ_PAIRS), 1.0, 6.0, ((0, 64), (1, 8))),
    }


def reference(integrals, amplitudes):
    return jnp.dot(integrals, amplitudes, preferred_element_type=jnp.float32)
```

```python
import functools

import jax
import jax.numpy as jnp
import numpy as np
from jax import lax
from jax.experimental import pallas as pl
from jax.experimental.pallas import tpu as pltpu
from jax.sharding import Mesh, PartitionSpec as P

AXES = ("yh", "z", "yl", "core", "x")
UNIT = 256


def moved(value, sizes, axes, where):
    shape = [sizes[a] for a in axes]
    perm = []
    for i in range(int(np.prod(shape))):
        place = dict(zip(axes, (int(v) for v in np.unravel_index(i, shape))))
        there = where(**place)
        perm.append((i, int(np.ravel_multi_index([there[a] for a in axes], shape))))
    return lax.ppermute(value, axes, perm)


def around_z(value, sizes, by):
    return moved(value, sizes, ("z",), lambda z: {"z": (z + by) % sizes["z"]})


def across_yl(value, sizes, mask):
    return moved(value, sizes, ("yl",), lambda yl: {"yl": yl ^ mask})


def regroup(value, sizes, second):
    def where(yh, yl, x):
        half = (x >> 1) ^ second
        return {"yh": yl >> 1, "yl": 2 * yh + (yl & 1), "x": 2 * (x & 1) + half}

    return moved(value, sizes, ("yh", "yl", "x"), where)


def product_kernel(place, w_ref, *refs):
    t_refs, out_ref = refs[:-1], refs[-1]
    for step, t_ref in enumerate(t_refs):
        t = t_ref[...]
        for rel in range(2):
            w = w_ref[place[2 * step + rel]]
            part = jnp.dot(w, t, preferred_element_type=jnp.float32)
            for block in range(4):
                cols = part[:, block * 128 : (block + 1) * 128]
                if step == 0:
                    out_ref[block, rel] = cols
                else:
                    out_ref[block, rel] += cols


def per_device(sizes, integrals, amplitudes):
    yh, z, yl, x = (lax.axis_index(a) for a in ("yh", "z", "yl", "x"))
    rows = integrals.shape[0]
    halves = jnp.stack([integrals[:, :UNIT], integrals[:, UNIT:]])
    high = x >> 1
    first = regroup(lax.dynamic_index_in_dim(halves, high, 0, False), sizes, 0)
    second = regroup(lax.dynamic_index_in_dim(halves, 1 - high, 0, False), sizes, 1)
    own = jnp.stack([first, second])
    by1 = across_yl(own, sizes, 1)
    by2 = across_yl(own, sizes, 2)
    by3 = across_yl(by1, sizes, 2)
    slab = lax.all_gather(jnp.stack([own, by1, by2, by3]), "core", axis=0)
    slab = slab.reshape(-1, rows, UNIT)
    up, down = [amplitudes], [amplitudes]
    for _ in range(3):
        up.append(around_z(up[-1], sizes, 1))
        down.append(around_z(down[-1], sizes, -1))
    up.append(around_z(up[-1], sizes, 1))
    tiles = up + down[1:]
    offsets = [-i for i in range(5)] + [1, 2, 3]
    place = []
    for offset in offsets:
        unit = (z + offset) % sizes["z"]
        u4, u3, u2 = unit >> 2, (unit >> 1) & 1, unit & 1
        for rel in range(2):
            m = yh ^ rel
            slot = ((m ^ (yl >> 1)) << 1) | (u4 ^ (yl & 1))
            place.append((u3 * 4 + slot) * 2 + (u2 ^ (x & 1)))
    place = jnp.stack(place).astype(jnp.int32)
    vmem = pl.BlockSpec(memory_space=pltpu.VMEM)
    part = pl.pallas_call(
        product_kernel,
        out_shape=jax.ShapeDtypeStruct((4, 2, rows, 128), jnp.float32),
        in_specs=[pl.BlockSpec(memory_space=pltpu.SMEM)] + [vmem] * 9,
        out_specs=vmem,
        compiler_params=pltpu.CompilerParams(vmem_limit_bytes=48 * 1024 * 1024),
    )(place, slab, *tiles)
    part = lax.all_to_all(part, "x", split_axis=0, concat_axis=0, tiled=True)
    total = part.sum(axis=0)
    other = moved(total[1], sizes, ("yh",), lambda yh: {"yh": 1 - yh})
    return total[0] + other


def solution(mesh):
    fine = Mesh(mesh.devices.reshape(2, 8, 4, 2, 4), AXES)
    sizes = dict(fine.shape)
    return jax.shard_map(
        functools.partial(per_device, sizes),
        mesh=fine,
        in_specs=(P(("yh", "z"), ("yl", "core", "x")), P(("yh", "z", "x"), ("yl", "core"))),
        out_specs=P(("yh", "z"), ("yl", "core", "x")),
        check_vma=False,
    )
```

```python
import functools

import jax
import jax.numpy as jnp
import numpy as np
from jax import lax
from jax.experimental import pallas as pl
from jax.experimental.pallas import tpu as pltpu
from jax.sharding import Mesh, PartitionSpec as P

AXES = ("yh", "z", "yl", "core", "x")
UNIT = 256


def moved(value, sizes, axes, where):
    shape = [sizes[a] for a in axes]
    perm = []
    for i in range(int(np.prod(shape))):
        place = dict(zip(axes, (int(v) for v in np.unravel_index(i, shape))))
        there = where(**place)
        perm.append((i, int(np.ravel_multi_index([there[a] for a in axes], shape))))
    return lax.ppermute(value, axes, perm)


def around_z(value, sizes):
    return moved(
        value, sizes, ("z", "core"), lambda z, core: {"z": (z + 1 - 2 * core) % sizes["z"], "core": core}
    )


def along_yl(value, sizes):
    return moved(value, sizes, ("yl",), lambda yl: {"yl": (yl + 1) % sizes["yl"]})


def core_swap(value, sizes):
    return moved(value, sizes, ("core",), lambda core: {"core": 1 - core})


def regroup(value, sizes, second):
    def where(yh, yl, x):
        half = (x >> 1) ^ second
        return {"yh": yl >> 1, "yl": 2 * yh + (yl & 1), "x": 2 * (x & 1) + half}

    return moved(value, sizes, ("yh", "yl", "x"), where)


def product_kernel(place, own_ref, other_ref, *refs):
    t_refs, out_ref = refs[:-1], refs[-1]
    for step, t_ref in enumerate(t_refs):
        t = t_ref[...]
        same = place[3 * step] == 1
        for rel in range(2):
            slot = place[3 * step + 1 + rel]
            w = jnp.where(same, own_ref[slot], other_ref[slot])
            part = jnp.dot(w, t, preferred_element_type=jnp.float32)
            for block in range(4):
                cols = part[:, block * 128 : (block + 1) * 128]
                if step == 0:
                    out_ref[block, rel] = cols
                else:
                    out_ref[block, rel] += cols


def per_device(sizes, integrals, amplitudes):
    yh, z, yl, core, x = (lax.axis_index(a) for a in AXES)
    rows = integrals.shape[0]
    tiles = [amplitudes]
    for _ in range(sizes["z"] - 1):
        tiles.append(around_z(tiles[-1], sizes))
    halves = jnp.stack([integrals[:, :UNIT], integrals[:, UNIT:]])
    high = x >> 1
    first = regroup(lax.dynamic_index_in_dim(halves, high, 0, False), sizes, 0)
    second = regroup(lax.dynamic_index_in_dim(halves, 1 - high, 0, False), sizes, 1)
    slabs = [jnp.stack([first, second])]
    for _ in range(sizes["yl"] - 1):
        slabs.append(along_yl(slabs[-1], sizes))
    own = jnp.concatenate(slabs)
    other = core_swap(own, sizes)
    place = []
    for step in range(sizes["z"]):
        unit = (z + step * (2 * core - 1)) % sizes["z"]
        u4, u3, u2 = unit >> 2, (unit >> 1) & 1, unit & 1
        place.append(jnp.where(u3 == core, 1, 0))
        for rel in range(2):
            source = 2 * (yh ^ rel) + u4
            place.append(((yl - source) % sizes["yl"]) * 2 + (u2 ^ (x & 1)))
    place = jnp.stack(place).astype(jnp.int32)
    vmem = pl.BlockSpec(memory_space=pltpu.VMEM)
    part = pl.pallas_call(
        product_kernel,
        out_shape=jax.ShapeDtypeStruct((4, 2, rows, 128), jnp.float32),
        in_specs=[pl.BlockSpec(memory_space=pltpu.SMEM)] + [vmem] * 10,
        out_specs=vmem,
        compiler_params=pltpu.CompilerParams(vmem_limit_bytes=48 * 1024 * 1024),
    )(place, own, other, *tiles)
    part = lax.all_to_all(part, "x", split_axis=0, concat_axis=0, tiled=True)
    total = part.sum(axis=0)
    other = moved(total[1], sizes, ("yh",), lambda yh: {"yh": 1 - yh})
    return total[0] + other


def solution(mesh):
    fine = Mesh(mesh.devices.reshape(2, 8, 4, 2, 4), AXES)
    sizes = dict(fine.shape)
    return jax.shard_map(
        functools.partial(per_device, sizes),
        mesh=fine,
        in_specs=(P(("yh", "z"), ("yl", "core", "x")), P(("yh", "z", "x"), ("yl", "core"))),
        out_specs=P(("yh", "z"), ("yl", "core", "x")),
        check_vma=False,
    )
```

```python
import functools

import jax
import jax.numpy as jnp
import numpy as np
from jax import lax
from jax.experimental import pallas as pl
from jax.experimental.pallas import tpu as pltpu
from jax.sharding import Mesh, PartitionSpec as P

AXES = ("yh", "z", "yl", "core", "x")
UNIT = 256


def moved(value, sizes, axes, where):
    shape = [sizes[a] for a in axes]
    perm = []
    for i in range(int(np.prod(shape))):
        place = dict(zip(axes, (int(v) for v in np.unravel_index(i, shape))))
        there = where(**place)
        perm.append((i, int(np.ravel_multi_index([there[a] for a in axes], shape))))
    return lax.ppermute(value, axes, perm)


def around_z(value, sizes, by):
    return moved(value, sizes, ("z",), lambda z: {"z": (z + by) % sizes["z"]})


def opposite_z(up, down, core, sizes):
    value = jnp.where(core == 0, up, down)
    return moved(
        value, sizes, ("z", "core"), lambda z, core: {"z": (z + 2 - 4 * core) % sizes["z"], "core": core}
    )


def along_yl(value, sizes, by):
    return moved(value, sizes, ("yl",), lambda yl: {"yl": (yl + by) % sizes["yl"]})


def core_swap(value, sizes):
    return moved(value, sizes, ("core",), lambda core: {"core": 1 - core})


def regroup(value, sizes, second):
    def where(yh, yl, x):
        half = (x >> 1) ^ second
        return {"yh": yl >> 1, "yl": 2 * yh + (yl & 1), "x": 2 * (x & 1) + half}

    return moved(value, sizes, ("yh", "yl", "x"), where)


def product_kernel(place, own_ref, other_ref, *refs):
    t_refs, out_ref = refs[:-1], refs[-1]
    for step, t_ref in enumerate(t_refs):
        t = t_ref[...]
        same = place[3 * step] == 1
        for rel in range(2):
            slot = place[3 * step + 1 + rel]
            w = jnp.where(same, own_ref[slot], other_ref[slot])
            part = jnp.dot(w, t, preferred_element_type=jnp.float32)
            for block in range(4):
                cols = part[:, block * 128 : (block + 1) * 128]
                if step == 0:
                    out_ref[block, rel] = cols
                else:
                    out_ref[block, rel] += cols


def per_device(sizes, integrals, amplitudes):
    yh, z, yl, core, x = (lax.axis_index(a) for a in AXES)
    rows = integrals.shape[0]
    tiles = {0: amplitudes}
    for by in (1, -1, 2, -2):
        tiles[-by] = around_z(amplitudes, sizes, by)
    tiles[-3] = around_z(tiles[-2], sizes, 1)
    tiles[3] = around_z(tiles[2], sizes, -1)
    tiles[4] = opposite_z(tiles[-2], tiles[2], core, sizes)
    halves = jnp.stack([integrals[:, :UNIT], integrals[:, UNIT:]])
    high = x >> 1
    first = regroup(lax.dynamic_index_in_dim(halves, high, 0, False), sizes, 0)
    second = regroup(lax.dynamic_index_in_dim(halves, 1 - high, 0, False), sizes, 1)
    slab = jnp.stack([first, second])
    own = jnp.concatenate([slab] + [along_yl(slab, sizes, by) for by in range(1, sizes["yl"])])
    other = core_swap(own, sizes)
    place = []
    for offset in tiles:
        unit = (z + offset) % sizes["z"]
        u4, u3, u2 = unit >> 2, (unit >> 1) & 1, unit & 1
        place.append(jnp.where(u3 == core, 1, 0))
        for rel in range(2):
            source = 2 * (yh ^ rel) + u4
            place.append(((yl - source) % sizes["yl"]) * 2 + (u2 ^ (x & 1)))
    place = jnp.stack(place).astype(jnp.int32)
    vmem = pl.BlockSpec(memory_space=pltpu.VMEM)
    part = pl.pallas_call(
        product_kernel,
        out_shape=jax.ShapeDtypeStruct((4, 2, rows, 128), jnp.float32),
        in_specs=[pl.BlockSpec(memory_space=pltpu.SMEM)] + [vmem] * 10,
        out_specs=vmem,
        compiler_params=pltpu.CompilerParams(vmem_limit_bytes=48 * 1024 * 1024),
    )(place, own, other, *tiles.values())
    part = lax.all_to_all(part, "x", split_axis=0, concat_axis=0, tiled=True)
    total = part.sum(axis=0)
    other = moved(total[1], sizes, ("yh",), lambda yh: {"yh": 1 - yh})
    return total[0] + other


def solution(mesh):
    fine = Mesh(mesh.devices.reshape(2, 8, 4, 2, 4), AXES)
    sizes = dict(fine.shape)
    return jax.shard_map(
        functools.partial(per_device, sizes),
        mesh=fine,
        in_specs=(P(("yh", "z"), ("yl", "core", "x")), P(("yh", "z", "x"), ("yl", "core"))),
        out_specs=P(("yh", "z"), ("yl", "core", "x")),
        check_vma=False,
    )
```

```python
import functools

import jax
import jax.numpy as jnp
import numpy as np
from jax import lax
from jax.experimental import pallas as pl
from jax.experimental.pallas import tpu as pltpu
from jax.sharding import Mesh, PartitionSpec as P

AXES = ("yh", "zh", "zl", "yl", "core", "x")
SHAPE = (2, 4, 2, 4, 2, 4)
SIZES = dict(zip(AXES, SHAPE))
UNIT = 256


def moved(value, axes, where):
    shape = [SIZES[a] for a in axes]
    perm = []
    for i in range(int(np.prod(shape))):
        place = dict(zip(axes, (int(v) for v in np.unravel_index(i, shape))))
        there = where(**place)
        perm.append((i, int(np.ravel_multi_index([there[a] for a in axes], shape))))
    return lax.ppermute(value, axes, perm)


def along_z(value, by):
    def where(zh, zl):
        z = (2 * zh + zl + by) % 8
        return {"zh": z >> 1, "zl": z & 1}

    return moved(value, ("zh", "zl"), where)


def regrouped(value, turned, second):
    def where(yh, yl, x):
        half = (x >> 1) ^ second
        return {"yh": yl >> 1, "yl": 2 * (yh ^ turned) + (yl & 1), "x": 2 * (x & 1) + half}

    return moved(value, ("yh", "yl", "x"), where)


def core_swap(value):
    return moved(value, ("core",), lambda core: {"core": 1 - core})


def product_kernel(rel, place, near_ref, far_ref, near2_ref, far2_ref, even_ref, up_ref, down_ref, out_ref):
    tiles = [even_ref.at[i] for i in range(4)] + [up_ref.at[i] for i in range(2)] + [down_ref.at[i] for i in range(2)]
    for step, t_ref in enumerate(tiles):
        same, near, slot = place[4 * step] == 1, place[4 * step + 1] == 1, place[4 * step + 2 + rel]
        w = jnp.where(
            same,
            jnp.where(near, near_ref[slot], far_ref[slot]),
            jnp.where(near, near2_ref[slot], far2_ref[slot]),
        )
        part = jnp.dot(w, t_ref[...], preferred_element_type=jnp.float32)
        for block in range(4):
            cols = part[:, block * 128 : (block + 1) * 128]
            if step == 0:
                out_ref[block] = cols
            else:
                out_ref[block] += cols


def product(rel, place, *operands):
    vmem = pl.BlockSpec(memory_space=pltpu.VMEM)
    return pl.pallas_call(
        functools.partial(product_kernel, rel),
        out_shape=jax.ShapeDtypeStruct((4, UNIT, 128), jnp.float32),
        in_specs=[pl.BlockSpec(memory_space=pltpu.SMEM)] + [vmem] * len(operands),
        out_specs=vmem,
        compiler_params=pltpu.CompilerParams(vmem_limit_bytes=40 * 1024 * 1024),
    )(place, *operands)


def over_depth(part):
    return lax.all_to_all(part, "x", split_axis=0, concat_axis=0, tiled=True).sum(axis=0)


def per_device(integrals, amplitudes):
    yh, zh, zl, yl, core, x = (lax.axis_index(a) for a in AXES)
    copies = jnp.broadcast_to(amplitudes[None], (4,) + amplitudes.shape)
    even = lax.all_to_all(copies, "zh", split_axis=0, concat_axis=0, tiled=True)
    from_up = along_z(even[:2], -1)
    from_down = along_z(even[2:], 1)
    halves = jnp.stack([integrals[:, :UNIT], integrals[:, UNIT:]])
    high = x >> 1
    picked = [lax.dynamic_index_in_dim(halves, high ^ second, 0, False) for second in (0, 1)]
    near = jnp.stack([regrouped(picked[second], turned, second) for turned in (0, 1) for second in (0, 1)])
    far = moved(near, ("yl",), lambda yl: {"yl": yl ^ 1})
    near2, far2 = core_swap(near), core_swap(far)
    place = []
    for their_zh, their_zl in [(i, zl) for i in range(4)] + [(i, 1 - zl) for i in range(4)]:
        u4, u3, u2 = their_zh >> 1, their_zh & 1, their_zl
        place += [jnp.where(core == u3, 1, 0), jnp.where((yl & 1) == u4, 1, 0)]
        place += [((yh ^ rel) ^ (yl >> 1)) * 2 + (u2 ^ (x & 1)) for rel in (0, 1)]
    place = jnp.stack(place).astype(jnp.int32)
    operands = (near, far, near2, far2, even, from_up, from_down)
    other = over_depth(product(1, place, *operands))
    other = moved(other, ("yh",), lambda yh: {"yh": 1 - yh})
    return over_depth(product(0, place, *operands)) + other


def solution(mesh):
    return jax.shard_map(
        per_device,
        mesh=Mesh(mesh.devices.reshape(SHAPE), AXES),
        in_specs=(P(("yh", "zh", "zl"), ("yl", "core", "x")), P(("yh", "zh", "zl", "x"), ("yl", "core"))),
        out_specs=P(("yh", "zh", "zl"), ("yl", "core", "x")),
        check_vma=False,
    )
```

```python
import functools

import jax
import jax.numpy as jnp
import numpy as np
from jax import lax
from jax.experimental import pallas as pl
from jax.experimental.pallas import tpu as pltpu
from jax.sharding import Mesh, PartitionSpec as P

AXES = ("yh", "z", "yl", "core", "x")
SHAPE = (2, 8, 4, 2, 4)
SIZES = dict(zip(AXES, SHAPE))
UNIT = 256


def moved(value, axes, where):
    shape = [SIZES[a] for a in axes]
    perm = []
    for i in range(int(np.prod(shape))):
        place = dict(zip(axes, (int(v) for v in np.unravel_index(i, shape))))
        there = where(**place)
        perm.append((i, int(np.ravel_multi_index([there[a] for a in axes], shape))))
    return lax.ppermute(value, axes, perm)


def regrouped(value, second):
    def where(yh, yl, x):
        half = (x >> 1) ^ second
        return {"yh": yl >> 1, "yl": 2 * yh + (yl & 1), "x": 2 * (x & 1) + half}

    return moved(value, ("yh", "yl", "x"), where)


def across_yl(value, mask):
    return moved(value, ("yl",), lambda yl: {"yl": yl ^ mask})


def core_swap(value):
    return moved(value, ("core",), lambda core: {"core": 1 - core})


def product_kernel(place, near_ref, far_ref, near2_ref, far2_ref, t_ref, out_ref):
    for unit in range(8):
        t = t_ref[unit]
        same, near = place[4 * unit] == 1, place[4 * unit + 1] == 1
        for rel in range(2):
            slot = place[4 * unit + 2 + rel]
            w = jnp.where(
                same,
                jnp.where(near, near_ref[slot], far_ref[slot]),
                jnp.where(near, near2_ref[slot], far2_ref[slot]),
            )
            part = jnp.dot(w, t, preferred_element_type=jnp.float32)
            for block in range(4):
                cols = part[:, block * 128 : (block + 1) * 128]
                if unit == 0:
                    out_ref[block, rel] = cols
                else:
                    out_ref[block, rel] += cols


def product(place, *operands):
    vmem = pl.BlockSpec(memory_space=pltpu.VMEM)
    return pl.pallas_call(
        product_kernel,
        out_shape=jax.ShapeDtypeStruct((4, 2, UNIT, 128), jnp.float32),
        in_specs=[pl.BlockSpec(memory_space=pltpu.SMEM)] + [vmem] * len(operands),
        out_specs=vmem,
        compiler_params=pltpu.CompilerParams(vmem_limit_bytes=40 * 1024 * 1024),
    )(place, *operands)


def per_device(integrals, amplitudes):
    yh, z, yl, core, x = (lax.axis_index(a) for a in AXES)
    copies = jnp.broadcast_to(amplitudes[None], (8,) + amplitudes.shape)
    tiles = lax.all_to_all(copies, "z", split_axis=0, concat_axis=0, tiled=True)
    halves = jnp.stack([integrals[:, :UNIT], integrals[:, UNIT:]])
    high = x >> 1
    own = jnp.stack([regrouped(lax.dynamic_index_in_dim(halves, high ^ i, 0, False), i) for i in (0, 1)])
    near = jnp.concatenate([own, across_yl(own, 2)])
    far = across_yl(near, 1)
    near2, far2 = core_swap(near), core_swap(far)
    place = []
    for unit in range(8):
        u4, u3, u2 = unit >> 2, (unit >> 1) & 1, unit & 1
        place += [jnp.where(core == u3, 1, 0), jnp.where((yl & 1) == u4, 1, 0)]
        place += [((yh ^ rel) ^ (yl >> 1)) * 2 + (u2 ^ (x & 1)) for rel in (0, 1)]
    place = jnp.stack(place).astype(jnp.int32)
    part = product(place, near, far, near2, far2, tiles)
    part = lax.all_to_all(part, "x", split_axis=0, concat_axis=0, tiled=True).sum(axis=0)
    return part[0] + moved(part[1], ("yh",), lambda yh: {"yh": 1 - yh})


def solution(mesh):
    return jax.shard_map(
        per_device,
        mesh=Mesh(mesh.devices.reshape(SHAPE), AXES),
        in_specs=(P(("yh", "z"), ("yl", "core", "x")), P(("yh", "z", "x"), ("yl", "core"))),
        out_specs=P(("yh", "z"), ("yl", "core", "x")),
        check_vma=False,
    )
```

```python
import jax
import jax.numpy as jnp
import numpy as np
from jax import lax
from jax.experimental import pallas as pl
from jax.experimental.pallas import tpu as pltpu
from jax.sharding import Mesh, PartitionSpec as P

AXES = ("yh", "zh", "zl", "yl", "core", "x")
SHAPE = (2, 4, 2, 4, 2, 4)
SIZES = dict(zip(AXES, SHAPE))
UNIT = 256


def moved(value, axes, where):
    shape = [SIZES[a] for a in axes]
    perm = []
    for i in range(int(np.prod(shape))):
        place = dict(zip(axes, (int(v) for v in np.unravel_index(i, shape))))
        there = where(**place)
        perm.append((i, int(np.ravel_multi_index([there[a] for a in axes], shape))))
    return lax.ppermute(value, axes, perm)


def aligned(value):
    def where(yh, zh, zl, core, x):
        return {"yh": core, "zh": 2 * (zh >> 1) + yh, "zl": x & 1, "core": zh & 1, "x": 2 * zl + (x >> 1)}

    return moved(value, ("yh", "zh", "zl", "core", "x"), where)


def along_z(value, by):
    def where(zh, zl):
        z = (2 * zh + zl + by) % 8
        return {"zh": z >> 1, "zl": z & 1}

    return moved(value, ("zh", "zl"), where)


def product_kernel(place, w_ref, even_ref, up_ref, down_ref, out_ref):
    core, parity = place[0], place[1]
    for i in range(4):
        u4, u5 = i >> 1, i & 1
        same, other = even_ref[i], (up_ref if i < 2 else down_ref)[i % 2]
        for rel in range(2):
            w = w_ref[4 * (core ^ rel) + 2 * u5 + u4]
            low, high = w[:, :UNIT], w[:, UNIT:]
            part = jnp.dot(jnp.where(parity == 0, low, high), same, preferred_element_type=jnp.float32)
            part += jnp.dot(jnp.where(parity == 0, high, low), other, preferred_element_type=jnp.float32)
            for block in range(4):
                cols = part[:, block * 128 : (block + 1) * 128]
                if i == 0:
                    out_ref[rel, block] = cols
                else:
                    out_ref[rel, block] += cols


def product(place, *operands):
    vmem = pl.BlockSpec(memory_space=pltpu.VMEM)
    return pl.pallas_call(
        product_kernel,
        out_shape=jax.ShapeDtypeStruct((2, 4, UNIT, 128), jnp.float32),
        in_specs=[pl.BlockSpec(memory_space=pltpu.SMEM)] + [vmem] * len(operands),
        out_specs=vmem,
        compiler_params=pltpu.CompilerParams(vmem_limit_bytes=40 * 1024 * 1024),
    )(place, *operands)


def to_all(value, axes):
    copies = jnp.broadcast_to(value[None], (int(np.prod([SIZES[a] for a in axes])),) + value.shape)
    return lax.all_to_all(copies, axes, split_axis=0, concat_axis=0, tiled=True)


def per_device(integrals, amplitudes):
    even = to_all(aligned(amplitudes), ("zh",))
    from_up = along_z(even[:2], -1)
    from_down = along_z(even[2:], 1)
    slab = to_all(integrals, ("yh", "yl"))
    place = jnp.stack([lax.axis_index("core"), lax.axis_index("zl")]).astype(jnp.int32)
    part = product(place, slab, even, from_up, from_down)
    part = part[0] + moved(part[1], ("core",), lambda core: {"core": 1 - core})
    part = lax.all_to_all(part, "x", split_axis=0, concat_axis=0, tiled=True).sum(axis=0)
    return moved(part, ("yh", "core"), lambda yh, core: {"yh": core, "core": yh})


def solution(mesh):
    return jax.shard_map(
        per_device,
        mesh=Mesh(mesh.devices.reshape(SHAPE), AXES),
        in_specs=(P(("yh", "zh", "zl"), ("yl", "core", "x")), P(("yh", "zh", "zl", "x"), ("yl", "core"))),
        out_specs=P(("yh", "zh", "zl"), ("yl", "core", "x")),
        check_vma=False,
    )
```

```python
import functools

import jax
import jax.numpy as jnp
import numpy as np
from jax import lax
from jax.experimental import pallas as pl
from jax.experimental.pallas import tpu as pltpu
from jax.sharding import Mesh, PartitionSpec as P

AXES = ("yh", "zh", "zl", "yl", "core", "x")
SHAPE = (2, 4, 2, 4, 2, 4)
SIZES = dict(zip(AXES, SHAPE))
UNIT = 256


def moved(value, axes, where):
    shape = [SIZES[a] for a in axes]
    perm = []
    for i in range(int(np.prod(shape))):
        place = dict(zip(axes, (int(v) for v in np.unravel_index(i, shape))))
        there = where(**place)
        perm.append((i, int(np.ravel_multi_index([there[a] for a in axes], shape))))
    return lax.ppermute(value, axes, perm)


def along_z(value, by):
    def where(zh, zl):
        z = (2 * zh + zl + by) % 8
        return {"zh": z >> 1, "zl": z & 1}

    return moved(value, ("zh", "zl"), where)


def regrouped(value, second):
    def where(yh, yl, x):
        half = (x >> 1) ^ second
        return {"yh": yl >> 1, "yl": 2 * yh + (yl & 1), "x": 2 * (x & 1) + half}

    return moved(value, ("yh", "yl", "x"), where)


def across_yl(value, mask):
    return moved(value, ("yl",), lambda yl: {"yl": yl ^ mask})


def core_swap(value):
    return moved(value, ("core",), lambda core: {"core": 1 - core})


def join_kernel(first_ref, second_ref, arrived_ref, out_ref):
    out_ref[:2] = first_ref[...]
    out_ref[2:] = second_ref[...]


def joined(first, second, arrived):
    vmem = pl.BlockSpec(memory_space=pltpu.VMEM)
    return pl.pallas_call(
        join_kernel,
        out_shape=jax.ShapeDtypeStruct((4,) + first.shape[1:], first.dtype),
        in_specs=[vmem] * 3,
        out_specs=vmem,
        compiler_params=pltpu.CompilerParams(vmem_limit_bytes=24 * 1024 * 1024),
    )(first, second, arrived)


def product_kernel(place, near_ref, far_ref, near2_ref, far2_ref, even_ref, up_ref, down_ref, out_ref):
    tiles = [even_ref.at[i] for i in range(4)] + [up_ref.at[i] for i in range(2)] + [down_ref.at[i] for i in range(2)]
    for unit, t_ref in enumerate(tiles):
        t = t_ref[...]
        same, near = place[4 * unit] == 1, place[4 * unit + 1] == 1
        for rel in range(2):
            slot = place[4 * unit + 2 + rel]
            w = jnp.where(
                same,
                jnp.where(near, near_ref[slot], far_ref[slot]),
                jnp.where(near, near2_ref[slot], far2_ref[slot]),
            )
            part = jnp.dot(w, t, preferred_element_type=jnp.float32)
            for block in range(4):
                cols = part[:, block * 128 : (block + 1) * 128]
                if unit == 0:
                    out_ref[block, rel] = cols
                else:
                    out_ref[block, rel] += cols


def product(place, *operands):
    vmem = pl.BlockSpec(memory_space=pltpu.VMEM)
    return pl.pallas_call(
        product_kernel,
        out_shape=jax.ShapeDtypeStruct((4, 2, UNIT, 128), jnp.float32),
        in_specs=[pl.BlockSpec(memory_space=pltpu.SMEM)] + [vmem] * len(operands),
        out_specs=vmem,
        compiler_params=pltpu.CompilerParams(vmem_limit_bytes=24 * 1024 * 1024),
    )(place, *operands)


def per_device(integrals, amplitudes):
    yh, zh, zl, yl, core, x = (lax.axis_index(a) for a in AXES)
    copies = jnp.broadcast_to(amplitudes[None], (4,) + amplitudes.shape)
    even = lax.all_to_all(copies, "zh", split_axis=0, concat_axis=0, tiled=True)
    from_up = along_z(even[:2], -1)
    from_down = along_z(even[2:], 1)
    halves = jnp.stack([integrals[:, :UNIT], integrals[:, UNIT:]])
    high = x >> 1
    own = jnp.stack([regrouped(lax.dynamic_index_in_dim(halves, high ^ i, 0, False), i) for i in (0, 1)])
    near = joined(own, across_yl(own, 2), even)
    far = across_yl(near, 1)
    near2, far2 = core_swap(near), core_swap(far)
    place = []
    for u4, u3, u2 in [(i >> 1, i & 1, zl) for i in range(4)] + [(i >> 1, i & 1, 1 - zl) for i in range(4)]:
        place += [jnp.where(core == u3, 1, 0), jnp.where((yl & 1) == u4, 1, 0)]
        place += [((yh ^ rel) ^ (yl >> 1)) * 2 + (u2 ^ (x & 1)) for rel in (0, 1)]
    place = jnp.stack(place).astype(jnp.int32)
    part = product(place, near, far, near2, far2, even, from_up, from_down)
    part = lax.all_to_all(part, "x", split_axis=0, concat_axis=0, tiled=True).sum(axis=0)
    return part[0] + moved(part[1], ("yh",), lambda yh: {"yh": 1 - yh})


def solution(mesh):
    return jax.shard_map(
        per_device,
        mesh=Mesh(mesh.devices.reshape(SHAPE), AXES),
        in_specs=(P(("yh", "zh", "zl"), ("yl", "core", "x")), P(("yh", "zh", "zl", "x"), ("yl", "core"))),
        out_specs=P(("yh", "zh", "zl"), ("yl", "core", "x")),
        check_vma=False,
    )
```

```python
import functools

import jax
import jax.numpy as jnp
import numpy as np
from jax import lax
from jax.experimental import pallas as pl
from jax.experimental.pallas import tpu as pltpu
from jax.sharding import Mesh, PartitionSpec as P

AXES = ("yh", "z", "yl", "core", "x")
SHAPE = (2, 8, 4, 2, 4)
SIZES = dict(zip(AXES, SHAPE))
UNIT = 256


def moved(value, axes, where):
    shape = [SIZES[a] for a in axes]
    perm = []
    for i in range(int(np.prod(shape))):
        place = dict(zip(axes, (int(v) for v in np.unravel_index(i, shape))))
        there = where(**place)
        perm.append((i, int(np.ravel_multi_index([there[a] for a in axes], shape))))
    return lax.ppermute(value, axes, perm)


def spread(value, mask):
    def where(yh, yl, core, x):
        half = (x >> 1) ^ core
        return {"yh": yl >> 1, "yl": (2 * yh + (yl & 1)) ^ mask, "core": core, "x": 2 * (x & 1) + half}

    return moved(value, ("yh", "yl", "core", "x"), where)


def core_swap(value):
    return moved(value, ("core",), lambda core: {"core": 1 - core})


def product_kernel(place, own_a, own_b, other_a, other_b, t_ref, out_ref):
    for unit in range(8):
        t = t_ref[unit]
        same = place[5 * unit] == 1
        for rel in range(2):
            first, slot = place[5 * unit + 1 + 2 * rel] == 1, place[5 * unit + 2 + 2 * rel]
            w = jnp.where(
                same,
                jnp.where(first, own_a[slot], own_b[slot]),
                jnp.where(first, other_a[slot], other_b[slot]),
            )
            part = jnp.dot(w, t, preferred_element_type=jnp.float32)
            for block in range(4):
                cols = part[:, block * 128 : (block + 1) * 128]
                if unit == 0:
                    out_ref[block, rel] = cols
                else:
                    out_ref[block, rel] += cols


def product(place, *operands):
    vmem = pl.BlockSpec(memory_space=pltpu.VMEM)
    return pl.pallas_call(
        product_kernel,
        out_shape=jax.ShapeDtypeStruct((4, 2, UNIT, 128), jnp.float32),
        in_specs=[pl.BlockSpec(memory_space=pltpu.SMEM)] + [vmem] * len(operands),
        out_specs=vmem,
        compiler_params=pltpu.CompilerParams(vmem_limit_bytes=40 * 1024 * 1024),
    )(place, *operands)


def per_device(integrals, amplitudes):
    yh, z, yl, core, x = (lax.axis_index(a) for a in AXES)
    copies = jnp.broadcast_to(amplitudes[None], (8,) + amplitudes.shape)
    tiles = lax.all_to_all(copies, "z", split_axis=0, concat_axis=0, tiled=True)
    both = lax.all_gather(integrals, "core", axis=0)
    half = lax.dynamic_slice_in_dim(both, ((x >> 1) ^ core) * UNIT, UNIT, 2)
    own_a = jnp.concatenate([spread(half, mask) for mask in (0, 1)])
    own_b = jnp.concatenate([spread(half, mask) for mask in (2, 3)])
    other_a, other_b = core_swap(own_a), core_swap(own_b)
    place = []
    for unit in range(8):
        u4, u3, u2 = unit >> 2, (unit >> 1) & 1, unit & 1
        place.append(jnp.where(u2 ^ (x & 1) == core, 1, 0))
        for rel in (0, 1):
            mask = yl ^ (2 * (yh ^ rel) + u4)
            place += [jnp.where(mask < 2, 1, 0), (mask & 1) * 2 + u3]
    place = jnp.stack(place).astype(jnp.int32)
    part = product(place, own_a, own_b, other_a, other_b, tiles)
    part = lax.all_to_all(part, "x", split_axis=0, concat_axis=0, tiled=True).sum(axis=0)
    return part[0] + moved(part[1], ("yh",), lambda yh: {"yh": 1 - yh})


def solution(mesh):
    return jax.shard_map(
        per_device,
        mesh=Mesh(mesh.devices.reshape(SHAPE), AXES),
        in_specs=(P(("yh", "z"), ("yl", "core", "x")), P(("yh", "z", "x"), ("yl", "core"))),
        out_specs=P(("yh", "z"), ("yl", "core", "x")),
        check_vma=False,
    )
```

```python
import functools

import jax
import jax.numpy as jnp
import numpy as np
from jax import lax
from jax.experimental import pallas as pl
from jax.experimental.pallas import tpu as pltpu
from jax.sharding import Mesh, PartitionSpec as P

AXES = ("yh", "z", "yl", "core", "x")
SHAPE = (2, 8, 4, 2, 4)
SIZES = dict(zip(AXES, SHAPE))
UNIT = 256


def moved(value, axes, where):
    shape = [SIZES[a] for a in axes]
    perm = []
    for i in range(int(np.prod(shape))):
        place = dict(zip(axes, (int(v) for v in np.unravel_index(i, shape))))
        there = where(**place)
        perm.append((i, int(np.ravel_multi_index([there[a] for a in axes], shape))))
    return lax.ppermute(value, axes, perm)


def spread(value, mask):
    def where(yh, yl, core, x):
        half = (x >> 1) ^ core ^ (mask & 1)
        return {"yh": yl >> 1, "yl": (2 * yh + (yl & 1)) ^ mask, "core": core, "x": 2 * (x & 1) + half}

    return moved(value, ("yh", "yl", "core", "x"), where)


def core_swap(value):
    return moved(value, ("core",), lambda core: {"core": 1 - core})


def product_kernel(place, own_a, own_b, other_a, other_b, t_ref, out_ref):
    for unit in range(8):
        t = t_ref[unit]
        for m in range(2):
            same, first, slot = (place[3 * (2 * unit + m) + i] for i in range(3))
            w = jnp.where(
                same == 1,
                jnp.where(first == 1, own_a[slot], own_b[slot]),
                jnp.where(first == 1, other_a[slot], other_b[slot]),
            )
            part = jnp.dot(w, t, preferred_element_type=jnp.float32)
            for block in range(4):
                cols = part[:, block * 128 : (block + 1) * 128]
                if unit == 0:
                    out_ref[4 * m + block] = cols
                else:
                    out_ref[4 * m + block] += cols


def product(place, *operands):
    vmem = pl.BlockSpec(memory_space=pltpu.VMEM)
    return pl.pallas_call(
        product_kernel,
        out_shape=jax.ShapeDtypeStruct((8, UNIT, 128), jnp.float32),
        in_specs=[pl.BlockSpec(memory_space=pltpu.SMEM)] + [vmem] * len(operands),
        out_specs=vmem,
        compiler_params=pltpu.CompilerParams(vmem_limit_bytes=40 * 1024 * 1024),
    )(place, *operands)


def per_device(integrals, amplitudes):
    yl, core, x = (lax.axis_index(a) for a in ("yl", "core", "x"))
    copies = jnp.broadcast_to(amplitudes[None], (8,) + amplitudes.shape)
    tiles = lax.all_to_all(copies, "z", split_axis=0, concat_axis=0, tiled=True)
    both = lax.all_gather(integrals, "core", axis=0)
    halves = [lax.dynamic_slice_in_dim(both, ((x >> 1) ^ core ^ i) * UNIT, UNIT, 2) for i in (0, 1)]
    own_a = jnp.concatenate([spread(halves[mask & 1], mask) for mask in (0, 1)])
    own_b = jnp.concatenate([spread(halves[mask & 1], mask) for mask in (2, 3)])
    other_a, other_b = core_swap(own_a), core_swap(own_b)
    place = []
    for unit in range(8):
        u4, u3, u2 = unit >> 2, (unit >> 1) & 1, unit & 1
        for m in (0, 1):
            mask = yl ^ (2 * m + u4)
            place.append(jnp.where(u2 ^ (x & 1) == core ^ (mask & 1), 1, 0))
            place += [jnp.where(mask < 2, 1, 0), (mask & 1) * 2 + u3]
    place = jnp.stack(place).astype(jnp.int32)
    part = product(place, own_a, own_b, other_a, other_b, tiles)
    return lax.all_to_all(part, ("yh", "x"), split_axis=0, concat_axis=0, tiled=True).sum(axis=0)


def solution(mesh):
    return jax.shard_map(
        per_device,
        mesh=Mesh(mesh.devices.reshape(SHAPE), AXES),
        in_specs=(P(("yh", "z"), ("yl", "core", "x")), P(("yh", "z", "x"), ("yl", "core"))),
        out_specs=P(("yh", "z"), ("yl", "core", "x")),
        check_vma=False,
    )
```

```python
import functools

import jax
import jax.numpy as jnp
import numpy as np
from jax import lax
from jax.experimental import pallas as pl
from jax.experimental.pallas import tpu as pltpu
from jax.sharding import Mesh, PartitionSpec as P

AXES = ("yh", "z", "yl", "core", "x")
SHAPE = (2, 8, 4, 2, 4)
SIZES = dict(zip(AXES, SHAPE))
UNIT = 256


def moved(value, axes, where):
    shape = [SIZES[a] for a in axes]
    perm = []
    for i in range(int(np.prod(shape))):
        place = dict(zip(axes, (int(v) for v in np.unravel_index(i, shape))))
        there = where(**place)
        perm.append((i, int(np.ravel_multi_index([there[a] for a in axes], shape))))
    return lax.ppermute(value, axes, perm)


def spread(value, mask):
    def where(yh, yl, core, x):
        half = (x >> 1) ^ core
        return {"yh": yl >> 1, "yl": (2 * yh + (yl & 1)) ^ mask, "core": core, "x": 2 * (x & 1) + half}

    return moved(value, ("yh", "yl", "core", "x"), where)


def core_swap(value):
    return moved(value, ("core",), lambda core: {"core": 1 - core})


def product_kernel(place, own_a, own_b, other_a, other_b, t_ref, out_ref):
    for unit in range(8):
        t = t_ref[unit]
        same = place[5 * unit] == 1
        for rel in range(2):
            first, slot = place[5 * unit + 1 + 2 * rel] == 1, place[5 * unit + 2 + 2 * rel]
            w = jnp.where(
                same,
                jnp.where(first, own_a[slot], own_b[slot]),
                jnp.where(first, other_a[slot], other_b[slot]),
            )
            part = jnp.dot(w, t, preferred_element_type=jnp.float32)
            for block in range(4):
                cols = part[:, block * 128 : (block + 1) * 128]
                if unit == 0:
                    out_ref[block, rel] = cols
                else:
                    out_ref[block, rel] += cols


def product(place, *operands):
    vmem = pl.BlockSpec(memory_space=pltpu.VMEM)
    return pl.pallas_call(
        product_kernel,
        out_shape=jax.ShapeDtypeStruct((4, 2, UNIT, 128), jnp.float32),
        in_specs=[pl.BlockSpec(memory_space=pltpu.SMEM)] + [vmem] * len(operands),
        out_specs=vmem,
        compiler_params=pltpu.CompilerParams(vmem_limit_bytes=40 * 1024 * 1024),
    )(place, *operands)


def per_device(integrals, amplitudes):
    yh, z, yl, core, x = (lax.axis_index(a) for a in AXES)
    copies = jnp.broadcast_to(amplitudes[None], (8,) + amplitudes.shape)
    tiles = lax.all_to_all(copies, "z", split_axis=0, concat_axis=0, tiled=True)
    both = lax.all_gather(integrals, "core", axis=0)
    half = lax.dynamic_slice_in_dim(both, ((x >> 1) ^ core) * UNIT, UNIT, 2)
    slabs = {mask: spread(half, mask) for mask in (0, 3, 1)}
    slabs[2] = moved(slabs[0], ("yl",), lambda yl: {"yl": yl ^ 2})
    own_a = jnp.concatenate([slabs[0], slabs[3]])
    own_b = jnp.concatenate([slabs[2], slabs[1]])
    other_a, other_b = core_swap(own_a), core_swap(own_b)
    place = []
    for unit in range(8):
        u4, u3, u2 = unit >> 2, (unit >> 1) & 1, unit & 1
        place.append(jnp.where(u2 ^ (x & 1) == core, 1, 0))
        for rel in (0, 1):
            mask = yl ^ (2 * (yh ^ rel) + u4)
            place += [jnp.where(mask >> 1 == mask & 1, 1, 0), (mask & 1) * 2 + u3]
    place = jnp.stack(place).astype(jnp.int32)
    part = product(place, own_a, own_b, other_a, other_b, tiles)
    part = lax.all_to_all(part, "x", split_axis=0, concat_axis=0, tiled=True).sum(axis=0)
    return part[0] + moved(part[1], ("yh",), lambda yh: {"yh": 1 - yh})


def solution(mesh):
    return jax.shard_map(
        per_device,
        mesh=Mesh(mesh.devices.reshape(SHAPE), AXES),
        in_specs=(P(("yh", "z"), ("yl", "core", "x")), P(("yh", "z", "x"), ("yl", "core"))),
        out_specs=P(("yh", "z"), ("yl", "core", "x")),
        check_vma=False,
    )
```

```python
import functools

import jax
import jax.numpy as jnp
import numpy as np
from jax import lax
from jax.experimental import pallas as pl
from jax.experimental.pallas import tpu as pltpu
from jax.sharding import Mesh, PartitionSpec as P

AXES = ("yh", "zh", "zl", "yl", "core", "x")
SHAPE = (2, 4, 2, 4, 2, 4)
SIZES = dict(zip(AXES, SHAPE))
UNIT = 256


def moved(value, axes, where):
    shape = [SIZES[a] for a in axes]
    perm = []
    for i in range(int(np.prod(shape))):
        place = dict(zip(axes, (int(v) for v in np.unravel_index(i, shape))))
        there = where(**place)
        perm.append((i, int(np.ravel_multi_index([there[a] for a in axes], shape))))
    return lax.ppermute(value, axes, perm)


def along_z(value, by):
    def where(zh, zl):
        z = (2 * zh + zl + by) % 8
        return {"zh": z >> 1, "zl": z & 1}

    return moved(value, ("zh", "zl"), where)


def spread(value, mask):
    def where(yh, yl, core, x):
        half = (x >> 1) ^ core
        return {"yh": yl >> 1, "yl": (2 * yh + (yl & 1)) ^ mask, "core": core, "x": 2 * (x & 1) + half}

    return moved(value, ("yh", "yl", "core", "x"), where)


def core_swap(value):
    return moved(value, ("core",), lambda core: {"core": 1 - core})


VMEM = pl.BlockSpec(memory_space=pltpu.VMEM)
PARAMS = pltpu.CompilerParams(vmem_limit_bytes=24 * 1024 * 1024)


def split_kernel(tiles_ref, slab_ref, low_ref, high_ref, out_ref):
    low_ref[...] = tiles_ref[:2]
    high_ref[...] = tiles_ref[2:]
    out_ref[...] = slab_ref[...]


def split(tiles, slab):
    half = jax.ShapeDtypeStruct((2,) + tiles.shape[1:], tiles.dtype)
    return pl.pallas_call(
        split_kernel,
        out_shape=(half, half, jax.ShapeDtypeStruct(slab.shape, slab.dtype)),
        in_specs=[VMEM] * 2,
        out_specs=[VMEM] * 3,
        compiler_params=PARAMS,
    )(tiles, slab)


def product_kernel(place, own_a, own_b, other_a, other_b, low_ref, high_ref, up_ref, down_ref, out_ref):
    tiles = [ref.at[i] for ref in (low_ref, high_ref, up_ref, down_ref) for i in range(2)]
    for unit, t_ref in enumerate(tiles):
        t = t_ref[...]
        same = place[5 * unit] == 1
        for rel in range(2):
            first, slot = place[5 * unit + 1 + 2 * rel] == 1, place[5 * unit + 2 + 2 * rel]
            w = jnp.where(
                same,
                jnp.where(first, own_a[slot], own_b[slot]),
                jnp.where(first, other_a[slot], other_b[slot]),
            )
            part = jnp.dot(w, t, preferred_element_type=jnp.float32)
            for block in range(4):
                cols = part[:, block * 128 : (block + 1) * 128]
                if unit == 0:
                    out_ref[block, rel] = cols
                else:
                    out_ref[block, rel] += cols


def product(place, *operands):
    return pl.pallas_call(
        product_kernel,
        out_shape=jax.ShapeDtypeStruct((4, 2, UNIT, 128), jnp.float32),
        in_specs=[pl.BlockSpec(memory_space=pltpu.SMEM)] + [VMEM] * len(operands),
        out_specs=VMEM,
        compiler_params=PARAMS,
    )(place, *operands)


def per_device(integrals, amplitudes):
    yh, zh, zl, yl, core, x = (lax.axis_index(a) for a in AXES)
    both = lax.all_gather(integrals, "core", axis=0)
    half = lax.dynamic_slice_in_dim(both, ((x >> 1) ^ core) * UNIT, UNIT, 2)
    slabs = {mask: spread(half, mask) for mask in (0, 3, 1)}
    copies = jnp.broadcast_to(amplitudes[None], (4,) + amplitudes.shape)
    tiles = lax.all_to_all(copies, "zh", split_axis=0, concat_axis=0, tiled=True)
    low, high, slabs[0] = split(tiles, slabs[0])
    from_up = along_z(low, -1)
    from_down = along_z(high, 1)
    slabs[2] = moved(slabs[0], ("yl",), lambda yl: {"yl": yl ^ 2})
    own_a = jnp.concatenate([slabs[0], slabs[3]])
    own_b = jnp.concatenate([slabs[2], slabs[1]])
    other_a, other_b = core_swap(own_a), core_swap(own_b)
    place = []
    for u4, u3, u2 in [(i >> 1, i & 1, u2) for u2 in (zl, 1 - zl) for i in range(4)]:
        place.append(jnp.where(u2 ^ (x & 1) == core, 1, 0))
        for rel in (0, 1):
            mask = yl ^ (2 * (yh ^ rel) + u4)
            place += [jnp.where(mask >> 1 == mask & 1, 1, 0), (mask & 1) * 2 + u3]
    place = jnp.stack(place).astype(jnp.int32)
    part = product(place, own_a, own_b, other_a, other_b, low, high, from_up, from_down)
    part = lax.all_to_all(part, "x", split_axis=0, concat_axis=0, tiled=True).sum(axis=0)
    return part[0] + moved(part[1], ("yh",), lambda yh: {"yh": 1 - yh})


def solution(mesh):
    return jax.shard_map(
        per_device,
        mesh=Mesh(mesh.devices.reshape(SHAPE), AXES),
        in_specs=(P(("yh", "zh", "zl"), ("yl", "core", "x")), P(("yh", "zh", "zl", "x"), ("yl", "core"))),
        out_specs=P(("yh", "zh", "zl"), ("yl", "core", "x")),
        check_vma=False,
    )
```

```python
import functools

import jax
import jax.numpy as jnp
import numpy as np
from jax import lax
from jax.experimental import pallas as pl
from jax.experimental.pallas import tpu as pltpu
from jax.sharding import Mesh, PartitionSpec as P

AXES = ("yh", "z", "yl", "core", "x")
SHAPE = (2, 8, 4, 2, 4)
SIZES = dict(zip(AXES, SHAPE))
UNIT = 256


def moved(value, axes, where):
    shape = [SIZES[a] for a in axes]
    perm = []
    for i in range(int(np.prod(shape))):
        place = dict(zip(axes, (int(v) for v in np.unravel_index(i, shape))))
        there = where(**place)
        perm.append((i, int(np.ravel_multi_index([there[a] for a in axes], shape))))
    return lax.ppermute(value, axes, perm)


def spread(value, mask):
    def where(yh, yl, core, x):
        half = (x >> 1) ^ core
        return {"yh": yl >> 1, "yl": (2 * yh + (yl & 1)) ^ mask, "core": core, "x": 2 * (x & 1) + half}

    return moved(value, ("yh", "yl", "core", "x"), where)


def core_swap(value):
    return moved(value, ("core",), lambda core: {"core": 1 - core})


def product_kernel(place, own_a, own_b, other_a, other_b, t_ref, mine_ref, theirs_ref):
    for unit in range(8):
        t = t_ref[unit]
        same = place[5 * unit] == 1
        for rel in range(2):
            first, slot = place[5 * unit + 1 + 2 * rel] == 1, place[5 * unit + 2 + 2 * rel]
            w = jnp.where(
                same,
                jnp.where(first, own_a[slot], own_b[slot]),
                jnp.where(first, other_a[slot], other_b[slot]),
            )
            part = jnp.dot(w, t, preferred_element_type=jnp.float32)
            for block in range(4):
                cols = part[:, block * 128 : (block + 1) * 128]
                out_ref = theirs_ref if rel else mine_ref
                if unit == 0:
                    out_ref[block] = cols
                else:
                    out_ref[block] += cols


VMEM = pl.BlockSpec(memory_space=pltpu.VMEM)
PARAMS = pltpu.CompilerParams(vmem_limit_bytes=40 * 1024 * 1024)


def product(place, *operands):
    out = jax.ShapeDtypeStruct((4, UNIT, 128), jnp.float32)
    return pl.pallas_call(
        product_kernel,
        out_shape=(out, out),
        in_specs=[pl.BlockSpec(memory_space=pltpu.SMEM)] + [VMEM] * len(operands),
        out_specs=(VMEM, VMEM),
        compiler_params=PARAMS,
    )(place, *operands)


def after_kernel(value_ref, first_ref, out_ref):
    out_ref[...] = value_ref[...]


def after(value, first):
    return pl.pallas_call(
        after_kernel,
        out_shape=jax.ShapeDtypeStruct(value.shape, value.dtype),
        in_specs=[VMEM, VMEM],
        out_specs=VMEM,
        compiler_params=PARAMS,
    )(value, first)


def over_depth(part):
    return lax.all_to_all(part, "x", split_axis=0, concat_axis=0, tiled=True).sum(axis=0)


def per_device(integrals, amplitudes):
    yh, z, yl, core, x = (lax.axis_index(a) for a in AXES)
    copies = jnp.broadcast_to(amplitudes[None], (8,) + amplitudes.shape)
    tiles = lax.all_to_all(copies, "z", split_axis=0, concat_axis=0, tiled=True)
    both = lax.all_gather(integrals, "core", axis=0)
    half = lax.dynamic_slice_in_dim(both, ((x >> 1) ^ core) * UNIT, UNIT, 2)
    slabs = {mask: spread(half, mask) for mask in (0, 3, 1)}
    slabs[2] = moved(slabs[0], ("yl",), lambda yl: {"yl": yl ^ 2})
    own_a = jnp.concatenate([slabs[0], slabs[3]])
    own_b = jnp.concatenate([slabs[2], slabs[1]])
    other_a, other_b = core_swap(own_a), core_swap(own_b)
    place = []
    for unit in range(8):
        u4, u3, u2 = unit >> 2, (unit >> 1) & 1, unit & 1
        place.append(jnp.where(u2 ^ (x & 1) == core, 1, 0))
        for rel in (0, 1):
            mask = yl ^ (2 * (yh ^ rel) + u4)
            place += [jnp.where(mask >> 1 == mask & 1, 1, 0), (mask & 1) * 2 + u3]
    place = jnp.stack(place).astype(jnp.int32)
    mine, theirs = product(place, own_a, own_b, other_a, other_b, tiles)
    theirs = over_depth(theirs)
    arriving = moved(theirs, ("yh",), lambda yh: {"yh": 1 - yh})
    return over_depth(after(mine, theirs)) + arriving


def solution(mesh):
    return jax.shard_map(
        per_device,
        mesh=Mesh(mesh.devices.reshape(SHAPE), AXES),
        in_specs=(P(("yh", "z"), ("yl", "core", "x")), P(("yh", "z", "x"), ("yl", "core"))),
        out_specs=P(("yh", "z"), ("yl", "core", "x")),
        check_vma=False,
    )
```

```python
import functools

import jax
import jax.numpy as jnp
import numpy as np
from jax import lax
from jax.experimental import pallas as pl
from jax.experimental.pallas import tpu as pltpu
from jax.sharding import Mesh, PartitionSpec as P

AXES = ("yh", "z", "yl", "core", "x")
SHAPE = (2, 8, 4, 2, 4)
SIZES = dict(zip(AXES, SHAPE))
UNIT = 256


def moved(value, axes, where):
    shape = [SIZES[a] for a in axes]
    perm = []
    for i in range(int(np.prod(shape))):
        place = dict(zip(axes, (int(v) for v in np.unravel_index(i, shape))))
        there = where(**place)
        perm.append((i, int(np.ravel_multi_index([there[a] for a in axes], shape))))
    return lax.ppermute(value, axes, perm)


def spread(value, mask):
    def where(yh, yl, core, x):
        half = (x >> 1) ^ core
        return {"yh": yl >> 1, "yl": (2 * yh + (yl & 1)) ^ mask, "core": core, "x": 2 * (x & 1) + half}

    return moved(value, ("yh", "yl", "core", "x"), where)


def core_swap(value):
    return moved(value, ("core",), lambda core: {"core": 1 - core})


def copies_kernel(tile_ref, out_ref, sems):
    copies = [pltpu.make_async_copy(tile_ref, out_ref.at[i], sems.at[i]) for i in range(8)]
    for copy in copies:
        copy.start()
    for copy in copies:
        copy.wait()


def copies_of(tile):
    return pl.pallas_call(
        copies_kernel,
        out_shape=jax.ShapeDtypeStruct((8,) + tile.shape, tile.dtype),
        in_specs=[pl.BlockSpec(memory_space=pl.ANY)],
        out_specs=pl.BlockSpec(memory_space=pl.ANY),
        scratch_shapes=[pltpu.SemaphoreType.DMA((8,))],
    )(tile)


def product_kernel(place, own_a, own_b, other_a, other_b, t_ref, out_ref):
    t = t_ref[...].reshape(8 * UNIT, t_ref.shape[2])
    for rel in range(2):
        blocks = []
        for unit in range(8):
            same = place[5 * unit] == 1
            first, slot = place[5 * unit + 1 + 2 * rel] == 1, place[5 * unit + 2 + 2 * rel]
            blocks.append(
                jnp.where(
                    same,
                    jnp.where(first, own_a[slot], own_b[slot]),
                    jnp.where(first, other_a[slot], other_b[slot]),
                )
            )
        part = jnp.dot(jnp.concatenate(blocks, axis=1), t, preferred_element_type=jnp.float32)
        for block in range(4):
            out_ref[block, rel] = part[:, block * 128 : (block + 1) * 128]


def product(place, *operands):
    vmem = pl.BlockSpec(memory_space=pltpu.VMEM)
    return pl.pallas_call(
        product_kernel,
        out_shape=jax.ShapeDtypeStruct((4, 2, UNIT, 128), jnp.float32),
        in_specs=[pl.BlockSpec(memory_space=pltpu.SMEM)] + [vmem] * len(operands),
        out_specs=vmem,
        compiler_params=pltpu.CompilerParams(vmem_limit_bytes=40 * 1024 * 1024),
    )(place, *operands)


def per_device(integrals, amplitudes):
    yh, z, yl, core, x = (lax.axis_index(a) for a in AXES)
    tiles = lax.all_to_all(copies_of(amplitudes), "z", split_axis=0, concat_axis=0, tiled=True)
    both = lax.all_gather(integrals, "core", axis=0)
    half = lax.dynamic_slice_in_dim(both, ((x >> 1) ^ core) * UNIT, UNIT, 2)
    slabs = {mask: spread(half, mask) for mask in (0, 3, 1)}
    slabs[2] = moved(slabs[0], ("yl",), lambda yl: {"yl": yl ^ 2})
    own_a = jnp.concatenate([slabs[0], slabs[3]])
    own_b = jnp.concatenate([slabs[2], slabs[1]])
    other_a, other_b = core_swap(own_a), core_swap(own_b)
    place = []
    for unit in range(8):
        u4, u3, u2 = unit >> 2, (unit >> 1) & 1, unit & 1
        place.append(jnp.where(u2 ^ (x & 1) == core, 1, 0))
        for rel in (0, 1):
            mask = yl ^ (2 * (yh ^ rel) + u4)
            place += [jnp.where(mask >> 1 == mask & 1, 1, 0), (mask & 1) * 2 + u3]
    place = jnp.stack(place).astype(jnp.int32)
    part = product(place, own_a, own_b, other_a, other_b, tiles)
    part = lax.all_to_all(part, "x", split_axis=0, concat_axis=0, tiled=True).sum(axis=0)
    return part[0] + moved(part[1], ("yh",), lambda yh: {"yh": 1 - yh})


def solution(mesh):
    return jax.shard_map(
        per_device,
        mesh=Mesh(mesh.devices.reshape(SHAPE), AXES),
        in_specs=(P(("yh", "z"), ("yl", "core", "x")), P(("yh", "z", "x"), ("yl", "core"))),
        out_specs=P(("yh", "z"), ("yl", "core", "x")),
        check_vma=False,
    )
```

```python
import functools

import jax
import jax.numpy as jnp
import numpy as np
from jax import lax
from jax.experimental import pallas as pl
from jax.experimental.pallas import tpu as pltpu
from jax.sharding import Mesh, PartitionSpec as P

AXES = ("yh", "z", "yl", "core", "x")
SHAPE = (2, 8, 4, 2, 4)
SIZES = dict(zip(AXES, SHAPE))
UNIT = 256


def moved(value, axes, where):
    shape = [SIZES[a] for a in axes]
    perm = []
    for i in range(int(np.prod(shape))):
        place = dict(zip(axes, (int(v) for v in np.unravel_index(i, shape))))
        there = where(**place)
        perm.append((i, int(np.ravel_multi_index([there[a] for a in axes], shape))))
    return lax.ppermute(value, axes, perm)


def spread(value, mask):
    def where(yh, yl, core, x):
        half = (x >> 1) ^ core
        return {"yh": yl >> 1, "yl": (2 * yh + (yl & 1)) ^ mask, "core": core, "x": 2 * (x & 1) + half}

    return moved(value, ("yh", "yl", "core", "x"), where)


def core_swap(value):
    return moved(value, ("core",), lambda core: {"core": 1 - core})


def copies_kernel(tile_ref, out_ref, sems):
    copies = [pltpu.make_async_copy(tile_ref, out_ref.at[i], sems.at[i]) for i in range(8)]
    for copy in copies:
        copy.start()
    for copy in copies:
        copy.wait()


def copies_of(tile):
    return pl.pallas_call(
        copies_kernel,
        out_shape=jax.ShapeDtypeStruct((8,) + tile.shape, tile.dtype),
        in_specs=[pl.BlockSpec(memory_space=pltpu.VMEM)],
        out_specs=pl.BlockSpec(memory_space=pl.ANY),
        scratch_shapes=[pltpu.SemaphoreType.DMA((8,))],
        compiler_params=pltpu.CompilerParams(vmem_limit_bytes=16 * 1024 * 1024),
    )(tile)


def product_kernel(place, own_a, own_b, other_a, other_b, t_ref, out_ref):
    t = t_ref[...].reshape(8 * UNIT, t_ref.shape[2])
    for rel in range(2):
        blocks = []
        for unit in range(8):
            same = place[5 * unit] == 1
            first, slot = place[5 * unit + 1 + 2 * rel] == 1, place[5 * unit + 2 + 2 * rel]
            blocks.append(
                jnp.where(
                    same,
                    jnp.where(first, own_a[slot], own_b[slot]),
                    jnp.where(first, other_a[slot], other_b[slot]),
                )
            )
        part = jnp.dot(jnp.concatenate(blocks, axis=1), t, preferred_element_type=jnp.float32)
        for block in range(4):
            out_ref[block, rel] = part[:, block * 128 : (block + 1) * 128]


def product(place, *operands):
    vmem = pl.BlockSpec(memory_space=pltpu.VMEM)
    return pl.pallas_call(
        product_kernel,
        out_shape=jax.ShapeDtypeStruct((4, 2, UNIT, 128), jnp.float32),
        in_specs=[pl.BlockSpec(memory_space=pltpu.SMEM)] + [vmem] * len(operands),
        out_specs=vmem,
        compiler_params=pltpu.CompilerParams(vmem_limit_bytes=16 * 1024 * 1024),
    )(place, *operands)


def per_device(integrals, amplitudes):
    yh, z, yl, core, x = (lax.axis_index(a) for a in AXES)
    tiles = lax.all_to_all(copies_of(amplitudes), "z", split_axis=0, concat_axis=0, tiled=True)
    both = lax.all_gather(integrals, "core", axis=0)
    half = lax.dynamic_slice_in_dim(both, ((x >> 1) ^ core) * UNIT, UNIT, 2)
    slabs = {mask: spread(half, mask) for mask in (0, 3, 1)}
    slabs[2] = moved(slabs[0], ("yl",), lambda yl: {"yl": yl ^ 2})
    own_a = jnp.concatenate([slabs[0], slabs[3]])
    own_b = jnp.concatenate([slabs[2], slabs[1]])
    other_a, other_b = core_swap(own_a), core_swap(own_b)
    place = []
    for unit in range(8):
        u4, u3, u2 = unit >> 2, (unit >> 1) & 1, unit & 1
        place.append(jnp.where(u2 ^ (x & 1) == core, 1, 0))
        for rel in (0, 1):
            mask = yl ^ (2 * (yh ^ rel) + u4)
            place += [jnp.where(mask >> 1 == mask & 1, 1, 0), (mask & 1) * 2 + u3]
    place = jnp.stack(place).astype(jnp.int32)
    part = product(place, own_a, own_b, other_a, other_b, tiles)
    part = lax.all_to_all(part, "x", split_axis=0, concat_axis=0, tiled=True).sum(axis=0)
    return part[0] + moved(part[1], ("yh",), lambda yh: {"yh": 1 - yh})


def solution(mesh):
    return jax.shard_map(
        per_device,
        mesh=Mesh(mesh.devices.reshape(SHAPE), AXES),
        in_specs=(P(("yh", "z"), ("yl", "core", "x")), P(("yh", "z", "x"), ("yl", "core"))),
        out_specs=P(("yh", "z"), ("yl", "core", "x")),
        check_vma=False,
    )
```

```python
import functools

import jax
import jax.numpy as jnp
import numpy as np
from jax import lax
from jax.experimental import pallas as pl
from jax.experimental.pallas import tpu as pltpu
from jax.sharding import Mesh, PartitionSpec as P

AXES = ("yh", "z", "yl", "core", "x")
SHAPE = (2, 8, 4, 2, 4)
SIZES = dict(zip(AXES, SHAPE))
UNIT = 256


def moved(value, axes, where):
    shape = [SIZES[a] for a in axes]
    perm = []
    for i in range(int(np.prod(shape))):
        place = dict(zip(axes, (int(v) for v in np.unravel_index(i, shape))))
        there = where(**place)
        perm.append((i, int(np.ravel_multi_index([there[a] for a in axes], shape))))
    return lax.ppermute(value, axes, perm)


def spread(value, mask):
    def where(yh, yl, core, x):
        half = (x >> 1) ^ core
        return {"yh": yl >> 1, "yl": (2 * yh + (yl & 1)) ^ mask, "core": core, "x": 2 * (x & 1) + half}

    return moved(value, ("yh", "yl", "core", "x"), where)


def core_swap(value):
    return moved(value, ("core",), lambda core: {"core": 1 - core})


def copies_kernel(tile_ref, out_ref, held, in_sems, out_sems):
    rows = tile_ref.shape[0] // 4
    reads = [
        pltpu.make_async_copy(tile_ref.at[pl.ds(i * rows, rows)], held.at[pl.ds(i * rows, rows)], in_sems.at[i])
        for i in range(4)
    ]
    for read in reads:
        read.start()
    writes = []
    for i, read in enumerate(reads):
        read.wait()
        part = pl.ds(i * rows, rows)
        for j in range(8):
            writes.append(pltpu.make_async_copy(held.at[part], out_ref.at[j, part], out_sems.at[i, j]))
            writes[-1].start()
    for write in writes:
        write.wait()


def copies_of(tile):
    return pl.pallas_call(
        copies_kernel,
        out_shape=jax.ShapeDtypeStruct((8,) + tile.shape, tile.dtype),
        in_specs=[pl.BlockSpec(memory_space=pltpu.HBM)],
        out_specs=pl.BlockSpec(memory_space=pltpu.HBM),
        scratch_shapes=[
            pltpu.VMEM(tile.shape, tile.dtype),
            pltpu.SemaphoreType.DMA((4,)),
            pltpu.SemaphoreType.DMA((4, 8)),
        ],
    )(tile)


def product_kernel(place, own_a, own_b, other_a, other_b, t_ref, out_ref):
    t = t_ref[...].reshape(8 * UNIT, t_ref.shape[2])
    for rel in range(2):
        blocks = []
        for unit in range(8):
            same = place[5 * unit] == 1
            first, slot = place[5 * unit + 1 + 2 * rel] == 1, place[5 * unit + 2 + 2 * rel]
            blocks.append(
                jnp.where(
                    same,
                    jnp.where(first, own_a[slot], own_b[slot]),
                    jnp.where(first, other_a[slot], other_b[slot]),
                )
            )
        part = jnp.dot(jnp.concatenate(blocks, axis=1), t, preferred_element_type=jnp.float32)
        for block in range(4):
            out_ref[block, rel] = part[:, block * 128 : (block + 1) * 128]


def product(place, *operands):
    vmem = pl.BlockSpec(memory_space=pltpu.VMEM)
    return pl.pallas_call(
        product_kernel,
        out_shape=jax.ShapeDtypeStruct((4, 2, UNIT, 128), jnp.float32),
        in_specs=[pl.BlockSpec(memory_space=pltpu.SMEM)] + [vmem] * len(operands),
        out_specs=vmem,
        compiler_params=pltpu.CompilerParams(vmem_limit_bytes=16 * 1024 * 1024),
    )(place, *operands)


def per_device(integrals, amplitudes):
    yh, z, yl, core, x = (lax.axis_index(a) for a in AXES)
    tiles = lax.all_to_all(copies_of(amplitudes), "z", split_axis=0, concat_axis=0, tiled=True)
    both = lax.all_gather(integrals, "core", axis=0)
    half = lax.dynamic_slice_in_dim(both, ((x >> 1) ^ core) * UNIT, UNIT, 2)
    slabs = {mask: spread(half, mask) for mask in (0, 3, 1)}
    slabs[2] = moved(slabs[0], ("yl",), lambda yl: {"yl": yl ^ 2})
    own_a = jnp.concatenate([slabs[0], slabs[3]])
    own_b = jnp.concatenate([slabs[2], slabs[1]])
    other_a, other_b = core_swap(own_a), core_swap(own_b)
    place = []
    for unit in range(8):
        u4, u3, u2 = unit >> 2, (unit >> 1) & 1, unit & 1
        place.append(jnp.where(u2 ^ (x & 1) == core, 1, 0))
        for rel in (0, 1):
            mask = yl ^ (2 * (yh ^ rel) + u4)
            place += [jnp.where(mask >> 1 == mask & 1, 1, 0), (mask & 1) * 2 + u3]
    place = jnp.stack(place).astype(jnp.int32)
    part = product(place, own_a, own_b, other_a, other_b, tiles)
    part = lax.all_to_all(part, "x", split_axis=0, concat_axis=0, tiled=True).sum(axis=0)
    return part[0] + moved(part[1], ("yh",), lambda yh: {"yh": 1 - yh})


def solution(mesh):
    return jax.shard_map(
        per_device,
        mesh=Mesh(mesh.devices.reshape(SHAPE), AXES),
        in_specs=(P(("yh", "z"), ("yl", "core", "x")), P(("yh", "z", "x"), ("yl", "core"))),
        out_specs=P(("yh", "z"), ("yl", "core", "x")),
        check_vma=False,
    )
```

```python
import functools

import jax
import jax.numpy as jnp
import numpy as np
from jax import lax
from jax.experimental import pallas as pl
from jax.experimental.pallas import tpu as pltpu
from jax.sharding import Mesh, PartitionSpec as P

AXES = ("yh", "z", "yl", "core", "x")
SHAPE = (2, 8, 4, 2, 4)
SIZES = dict(zip(AXES, SHAPE))
UNIT = 256


def moved(value, axes, where):
    shape = [SIZES[a] for a in axes]
    perm = []
    for i in range(int(np.prod(shape))):
        place = dict(zip(axes, (int(v) for v in np.unravel_index(i, shape))))
        there = where(**place)
        perm.append((i, int(np.ravel_multi_index([there[a] for a in axes], shape))))
    return lax.ppermute(value, axes, perm)


def spread(value, mask):
    def where(yh, yl, core, x):
        half = (x >> 1) ^ core
        return {"yh": yl >> 1, "yl": (2 * yh + (yl & 1)) ^ mask, "core": core, "x": 2 * (x & 1) + half}

    return moved(value, ("yh", "yl", "core", "x"), where)


def core_swap(value):
    return moved(value, ("core",), lambda core: {"core": 1 - core})


def copies_kernel(tile_ref, out_ref, held, in_sems, out_sems):
    rows = tile_ref.shape[0] // 4
    reads = [
        pltpu.make_async_copy(tile_ref.at[pl.ds(i * rows, rows)], held.at[pl.ds(i * rows, rows)], in_sems.at[i])
        for i in range(4)
    ]
    for read in reads:
        read.start()
    writes = []
    for i, read in enumerate(reads):
        read.wait()
        part = pl.ds(i * rows, rows)
        for j in range(8):
            writes.append(pltpu.make_async_copy(held.at[part], out_ref.at[j, part], out_sems.at[i, j]))
            writes[-1].start()
    for write in writes:
        write.wait()


def copies_of(tile):
    return pl.pallas_call(
        copies_kernel,
        out_shape=jax.ShapeDtypeStruct((8,) + tile.shape, tile.dtype),
        in_specs=[pl.BlockSpec(memory_space=pltpu.HBM)],
        out_specs=pl.BlockSpec(memory_space=pltpu.HBM),
        scratch_shapes=[
            pltpu.VMEM(tile.shape, tile.dtype),
            pltpu.SemaphoreType.DMA((4,)),
            pltpu.SemaphoreType.DMA((4, 8)),
        ],
    )(tile)


VMEM = pl.BlockSpec(memory_space=pltpu.VMEM)
PARAMS = pltpu.CompilerParams(vmem_limit_bytes=16 * 1024 * 1024)


def order_kernel(place, own_a, own_b, other_a, other_b, out_ref):
    for unit in range(8):
        same = place[5 * unit] == 1
        for rel in range(2):
            first, slot = place[5 * unit + 1 + 2 * rel] == 1, place[5 * unit + 2 + 2 * rel]
            out_ref[rel * UNIT : (rel + 1) * UNIT, unit * UNIT : (unit + 1) * UNIT] = jnp.where(
                same,
                jnp.where(first, own_a[slot], own_b[slot]),
                jnp.where(first, other_a[slot], other_b[slot]),
            )


def ordered(place, *operands):
    return pl.pallas_call(
        order_kernel,
        out_shape=jax.ShapeDtypeStruct((2 * UNIT, 8 * UNIT), jnp.bfloat16),
        in_specs=[pl.BlockSpec(memory_space=pltpu.SMEM)] + [VMEM] * len(operands),
        out_specs=VMEM,
        compiler_params=PARAMS,
    )(place, *operands)


def product_kernel(w_ref, t_ref, out_ref):
    t = t_ref[...].reshape(8 * UNIT, t_ref.shape[2])
    for rel in range(2):
        part = jnp.dot(w_ref[rel * UNIT : (rel + 1) * UNIT, :], t, preferred_element_type=jnp.float32)
        for block in range(4):
            out_ref[block, rel] = part[:, block * 128 : (block + 1) * 128]


def product(slab, tiles):
    return pl.pallas_call(
        product_kernel,
        out_shape=jax.ShapeDtypeStruct((4, 2, UNIT, 128), jnp.float32),
        in_specs=[VMEM, VMEM],
        out_specs=VMEM,
        compiler_params=PARAMS,
    )(slab, tiles)


def per_device(integrals, amplitudes):
    yh, z, yl, core, x = (lax.axis_index(a) for a in AXES)
    tiles = lax.all_to_all(copies_of(amplitudes), "z", split_axis=0, concat_axis=0, tiled=True)
    both = lax.all_gather(integrals, "core", axis=0)
    half = lax.dynamic_slice_in_dim(both, ((x >> 1) ^ core) * UNIT, UNIT, 2)
    slabs = {mask: spread(half, mask) for mask in (0, 3, 1)}
    slabs[2] = moved(slabs[0], ("yl",), lambda yl: {"yl": yl ^ 2})
    own_a = jnp.concatenate([slabs[0], slabs[3]])
    own_b = jnp.concatenate([slabs[2], slabs[1]])
    other_a, other_b = core_swap(own_a), core_swap(own_b)
    place = []
    for unit in range(8):
        u4, u3, u2 = unit >> 2, (unit >> 1) & 1, unit & 1
        place.append(jnp.where(u2 ^ (x & 1) == core, 1, 0))
        for rel in (0, 1):
            mask = yl ^ (2 * (yh ^ rel) + u4)
            place += [jnp.where(mask >> 1 == mask & 1, 1, 0), (mask & 1) * 2 + u3]
    place = jnp.stack(place).astype(jnp.int32)
    part = product(ordered(place, own_a, own_b, other_a, other_b), tiles)
    part = lax.all_to_all(part, "x", split_axis=0, concat_axis=0, tiled=True).sum(axis=0)
    return part[0] + moved(part[1], ("yh",), lambda yh: {"yh": 1 - yh})


def solution(mesh):
    return jax.shard_map(
        per_device,
        mesh=Mesh(mesh.devices.reshape(SHAPE), AXES),
        in_specs=(P(("yh", "z"), ("yl", "core", "x")), P(("yh", "z", "x"), ("yl", "core"))),
        out_specs=P(("yh", "z"), ("yl", "core", "x")),
        check_vma=False,
    )
```

```python
import functools

import jax
import jax.numpy as jnp
import numpy as np
from jax import lax
from jax.experimental import pallas as pl
from jax.experimental.pallas import tpu as pltpu
from jax.sharding import Mesh, PartitionSpec as P

AXES = ("yh", "z", "yl", "core", "x")
SHAPE = (2, 8, 4, 2, 4)
SIZES = dict(zip(AXES, SHAPE))
UNIT = 256


def moved(value, axes, where):
    shape = [SIZES[a] for a in axes]
    perm = []
    for i in range(int(np.prod(shape))):
        place = dict(zip(axes, (int(v) for v in np.unravel_index(i, shape))))
        there = where(**place)
        perm.append((i, int(np.ravel_multi_index([there[a] for a in axes], shape))))
    return lax.ppermute(value, axes, perm)


def spread(value, mask):
    def where(yh, yl, core, x):
        half = (x >> 1) ^ core
        return {"yh": yl >> 1, "yl": (2 * yh + (yl & 1)) ^ mask, "core": core, "x": 2 * (x & 1) + half}

    return moved(value, ("yh", "yl", "core", "x"), where)


def core_swap(value):
    return moved(value, ("core",), lambda core: {"core": 1 - core})


def copies_kernel(tile_ref, out_ref, held, in_sems, out_sems):
    rows = tile_ref.shape[0] // 4
    reads = [
        pltpu.make_async_copy(tile_ref.at[pl.ds(i * rows, rows)], held.at[pl.ds(i * rows, rows)], in_sems.at[i])
        for i in range(4)
    ]
    for read in reads:
        read.start()
    writes = []
    for i, read in enumerate(reads):
        read.wait()
        part = pl.ds(i * rows, rows)
        for j in range(8):
            writes.append(pltpu.make_async_copy(held.at[part], out_ref.at[j, part], out_sems.at[i, j]))
            writes[-1].start()
    for write in writes:
        write.wait()


def copies_of(tile):
    return pl.pallas_call(
        copies_kernel,
        out_shape=jax.ShapeDtypeStruct((8,) + tile.shape, tile.dtype),
        in_specs=[pl.BlockSpec(memory_space=pltpu.HBM)],
        out_specs=pl.BlockSpec(memory_space=pltpu.HBM),
        scratch_shapes=[
            pltpu.VMEM(tile.shape, tile.dtype),
            pltpu.SemaphoreType.DMA((4,)),
            pltpu.SemaphoreType.DMA((4, 8)),
        ],
    )(tile)


def product_kernel(place, own_a, own_b, other_a, other_b, t_ref, out_ref):
    t = t_ref[...].reshape(8 * UNIT, t_ref.shape[2])
    for rel in range(2):
        blocks = []
        for unit in range(8):
            same = place[5 * unit] == 1
            first, slot = place[5 * unit + 1 + 2 * rel] == 1, place[5 * unit + 2 + 2 * rel]
            blocks.append(
                jnp.where(
                    same,
                    jnp.where(first, own_a[slot], own_b[slot]),
                    jnp.where(first, other_a[slot], other_b[slot]),
                )
            )
        part = jnp.dot(jnp.concatenate(blocks, axis=1), t, preferred_element_type=jnp.float32)
        for block in range(4):
            out_ref[block, rel] = part[:, block * 128 : (block + 1) * 128]


def product(place, *operands):
    vmem = pl.BlockSpec(memory_space=pltpu.VMEM)
    return pl.pallas_call(
        product_kernel,
        out_shape=jax.ShapeDtypeStruct((4, 2, UNIT, 128), jnp.float32),
        in_specs=[pl.BlockSpec(memory_space=pltpu.SMEM)] + [vmem] * len(operands),
        out_specs=vmem,
        compiler_params=pltpu.CompilerParams(vmem_limit_bytes=16 * 1024 * 1024),
    )(place, *operands)


def per_device(integrals, amplitudes):
    yh, z, yl, core, x = (lax.axis_index(a) for a in AXES)
    tiles = lax.all_to_all(copies_of(amplitudes), "z", split_axis=0, concat_axis=0, tiled=True)
    both = lax.all_gather(integrals, "core", axis=0)
    half = lax.dynamic_slice_in_dim(both, ((x >> 1) ^ core) * UNIT, UNIT, 2)
    slabs = {mask: spread(half, mask) for mask in (0, 3)}
    slabs[2] = moved(slabs[0], ("yl",), lambda yl: {"yl": yl ^ 2})
    slabs[1] = moved(slabs[0], ("yl",), lambda yl: {"yl": yl ^ 1})
    own_a = jnp.concatenate([slabs[0], slabs[3]])
    own_b = jnp.concatenate([slabs[2], slabs[1]])
    other_a, other_b = core_swap(own_a), core_swap(own_b)
    place = []
    for unit in range(8):
        u4, u3, u2 = unit >> 2, (unit >> 1) & 1, unit & 1
        place.append(jnp.where(u2 ^ (x & 1) == core, 1, 0))
        for rel in (0, 1):
            mask = yl ^ (2 * (yh ^ rel) + u4)
            place += [jnp.where(mask >> 1 == mask & 1, 1, 0), (mask & 1) * 2 + u3]
    place = jnp.stack(place).astype(jnp.int32)
    part = product(place, own_a, own_b, other_a, other_b, tiles)
    part = lax.all_to_all(part, "x", split_axis=0, concat_axis=0, tiled=True).sum(axis=0)
    return part[0] + moved(part[1], ("yh",), lambda yh: {"yh": 1 - yh})


def solution(mesh):
    return jax.shard_map(
        per_device,
        mesh=Mesh(mesh.devices.reshape(SHAPE), AXES),
        in_specs=(P(("yh", "z"), ("yl", "core", "x")), P(("yh", "z", "x"), ("yl", "core"))),
        out_specs=P(("yh", "z"), ("yl", "core", "x")),
        check_vma=False,
    )
```

```python
import functools

import jax
import jax.numpy as jnp
import numpy as np
from jax import lax
from jax.experimental import pallas as pl
from jax.experimental.pallas import tpu as pltpu
from jax.sharding import Mesh, PartitionSpec as P

AXES = ("yh", "z", "yl", "core", "x")
SHAPE = (2, 8, 4, 2, 4)
SIZES = dict(zip(AXES, SHAPE))
UNIT = 256


def moved(value, axes, where):
    shape = [SIZES[a] for a in axes]
    perm = []
    for i in range(int(np.prod(shape))):
        place = dict(zip(axes, (int(v) for v in np.unravel_index(i, shape))))
        there = where(**place)
        perm.append((i, int(np.ravel_multi_index([there[a] for a in axes], shape))))
    return lax.ppermute(value, axes, perm)


def spread(value, mask):
    def where(yh, yl, core, x):
        half = (x >> 1) ^ core
        return {"yh": yl >> 1, "yl": (2 * yh + (yl & 1)) ^ mask, "core": core, "x": 2 * (x & 1) + half}

    return moved(value, ("yh", "yl", "core", "x"), where)


def core_swap(value):
    return moved(value, ("core",), lambda core: {"core": 1 - core})


def copies_kernel(tile_ref, out_ref, held, in_sems, out_sems):
    rows = tile_ref.shape[0] // 4
    reads = [
        pltpu.make_async_copy(tile_ref.at[pl.ds(i * rows, rows)], held.at[pl.ds(i * rows, rows)], in_sems.at[i])
        for i in range(4)
    ]
    for read in reads:
        read.start()
    writes = []
    for i, read in enumerate(reads):
        read.wait()
        part = pl.ds(i * rows, rows)
        for j in range(8):
            writes.append(pltpu.make_async_copy(held.at[part], out_ref.at[j, part], out_sems.at[i, j]))
            writes[-1].start()
    for write in writes:
        write.wait()


def copies_of(tile):
    return pl.pallas_call(
        copies_kernel,
        out_shape=jax.ShapeDtypeStruct((8,) + tile.shape, tile.dtype),
        in_specs=[pl.BlockSpec(memory_space=pltpu.HBM)],
        out_specs=pl.BlockSpec(memory_space=pltpu.HBM),
        scratch_shapes=[
            pltpu.VMEM(tile.shape, tile.dtype),
            pltpu.SemaphoreType.DMA((4,)),
            pltpu.SemaphoreType.DMA((4, 8)),
        ],
    )(tile)


def product_kernel(place, own_a, own_b, other_a, other_b, t_ref, out_ref):
    t = t_ref[...].reshape(8 * UNIT, t_ref.shape[2])
    for rel in range(2):
        blocks = []
        for unit in range(8):
            same = place[5 * unit] == 1
            first, slot = place[5 * unit + 1 + 2 * rel] == 1, place[5 * unit + 2 + 2 * rel]
            blocks.append(
                jnp.where(
                    same,
                    jnp.where(first, own_a[slot], own_b[slot]),
                    jnp.where(first, other_a[slot], other_b[slot]),
                )
            )
        part = jnp.dot(jnp.concatenate(blocks, axis=1), t, preferred_element_type=jnp.float32)
        for block in range(4):
            out_ref[block, rel] = part[:, block * 128 : (block + 1) * 128]


def product(place, *operands):
    vmem = pl.BlockSpec(memory_space=pltpu.VMEM)
    return pl.pallas_call(
        product_kernel,
        out_shape=jax.ShapeDtypeStruct((4, 2, UNIT, 128), jnp.float32),
        in_specs=[pl.BlockSpec(memory_space=pltpu.SMEM)] + [vmem] * len(operands),
        out_specs=vmem,
        compiler_params=pltpu.CompilerParams(vmem_limit_bytes=16 * 1024 * 1024),
    )(place, *operands)


def per_device(integrals, amplitudes):
    yh, z, yl, core, x = (lax.axis_index(a) for a in AXES)
    tiles = lax.all_to_all(copies_of(amplitudes), "z", split_axis=0, concat_axis=0, tiled=True)
    both = lax.all_gather(integrals, "core", axis=0)
    half = lax.dynamic_slice_in_dim(both, ((x >> 1) ^ core) * UNIT, UNIT, 2)
    slabs = {0: spread(half, 0)}
    for mask in (3, 2, 1):
        slabs[mask] = moved(slabs[0], ("yl",), lambda yl: {"yl": yl ^ mask})
    own_a = jnp.concatenate([slabs[0], slabs[3]])
    own_b = jnp.concatenate([slabs[2], slabs[1]])
    other_a, other_b = core_swap(own_a), core_swap(own_b)
    place = []
    for unit in range(8):
        u4, u3, u2 = unit >> 2, (unit >> 1) & 1, unit & 1
        place.append(jnp.where(u2 ^ (x & 1) == core, 1, 0))
        for rel in (0, 1):
            mask = yl ^ (2 * (yh ^ rel) + u4)
            place += [jnp.where(mask >> 1 == mask & 1, 1, 0), (mask & 1) * 2 + u3]
    place = jnp.stack(place).astype(jnp.int32)
    part = product(place, own_a, own_b, other_a, other_b, tiles)
    part = lax.all_to_all(part, "x", split_axis=0, concat_axis=0, tiled=True).sum(axis=0)
    return part[0] + moved(part[1], ("yh",), lambda yh: {"yh": 1 - yh})


def solution(mesh):
    return jax.shard_map(
        per_device,
        mesh=Mesh(mesh.devices.reshape(SHAPE), AXES),
        in_specs=(P(("yh", "z"), ("yl", "core", "x")), P(("yh", "z", "x"), ("yl", "core"))),
        out_specs=P(("yh", "z"), ("yl", "core", "x")),
        check_vma=False,
    )
```
